768 devices in a mesh: band: 48 (over z, y_hi), lev: 4 (over y_lo, core), grp: 4 (over x).
Axes of the slice: x: 4, y: 8 (y_hi: 4, y_lo: 2; y = y_hi * 2 + y_lo), z: 12, core: 2. Of those that a mesh axis runs over, the one named last changes fastest.
Arguments:
- fourier: bfloat16 [3, 8, 2, 2, 4, 288, 1152], P(None, 'lev', None, None, 'grp', 'band'), may hold values from -6 to 6
- legendre: bfloat16 [1152, 2, 576, 4, 288], P('band', None, 'lev', 'grp'), may hold values from -0.1875 to 0.1875
- lat_points: int32 [4, 288], P('grp', 'band'), may hold values from 20 to 4624, as said below
- wave_slots: int32 [1152], replicated, may hold values from 0 to 1151, as said below
- vertical: float32 [8, 8], replicated, may hold values from -2 to 2
Outputs:
- spectral: bfloat16 [1152, 2, 4, 8, 2, 576], P('band', None, None, None, None, ('lev', 'grp'))
The draws below stay inside these ranges and needn't reach their ends.
Inputs may be any that keep to these rules, and one draw needn't show every extreme that they name: `lat_points`: the values are 20 + 4 i for i = 0 .. 1151, each once (octahedral point counts of the latitude pairs, spread over devices). `wave_slots`: every wavenumber appears once; slots 2 i and 2 i + 1 hold wavenumbers m and 1151 - m.
All inputs are finite; a program needn't handle non-finite values.
Results may differ from the reference program's by a relative error of at most 0.0053.
Values may be sent and summed in bfloat16 or wider, within the bound.
A program may use at most 64 MiB of HBM per device.

```python
import jax
import jax.numpy as jnp
from jax import lax

M = 1152
LEVELS = 8
FIELDS = 3
N_GRP = 4


def draw_lat_points(key, part):
    order = jax.random.permutation(jax.random.fold_in(key, 11), M).astype(jnp.int32)
    return (20 + 4 * order).astype(jnp.int32).reshape(N_GRP, M // N_GRP)


def draw_wave_slots(key, part):
    lower = jax.random.permutation(jax.random.fold_in(key, 23), M // 2).astype(jnp.int32)
    return jnp.stack([lower, M - 1 - lower], axis=1).reshape(M).astype(jnp.int32)


def raised(values, stream_key, source, target, shards_of, factor):
    owner, partner = [(jnp.arange(values.shape[position]) // (values.shape[position] // shards_of)).reshape([-1 if axis == position else 1 for axis in range(values.ndim)]) for position in (source, target)]
    chosen = jax.random.permutation(stream_key, shards_of)[partner]
    strong = (owner == chosen) | (owner == (partner + shards_of // 2) % shards_of)
    return jnp.where(strong, factor * values, values)


def level_of(rng, extent, split, low, largest):
    loudness = 1.0
    for dim, shards_of in split:
        draws = jax.random.uniform(jax.random.fold_in(jax.random.fold_in(rng, 6), dim), (shards_of,), jnp.float32, low / len(split), largest / len(split))
        loudness = loudness * jnp.repeat(jnp.exp(draws), extent[dim] // shards_of).reshape((-1,) + (1,) * (len(extent) - 1 - dim))
    return loudness


def bell_draw(stream_key, extent, scale, bound, split=(), held_as=jnp.bfloat16):
    drawn = jax.random.normal(stream_key, extent, jnp.float32) * scale
    if len(split) > 0:
        drawn = level_of(stream_key, extent, split, -0.22, 0.18) * drawn
    return jnp.clip(drawn, min=-bound, max=bound).astype(held_as)


def gaussian_with(key, dims, spread, reach, cuts, heavy, kind=jnp.bfloat16):
    result = spread * jax.random.normal(key, dims, jnp.float32)
    if cuts:
        result = result * level_of(key, dims, cuts, -0.22, 0.18)
    return jnp.clip(raised(result, jax.random.fold_in(key, 3), *heavy), -reach, reach).astype(kind)


def setup_inputs(seed: int = 0) -> dict:
    keys = jax.random.split(jax.random.key(seed), 6)
    fourier = bell_draw(keys[0], (FIELDS, LEVELS, 2, 2, N_GRP, M // N_GRP, M), 1.0, 6.0, ((1, 4), (4, 4), (5, 48)))
    legendre = gaussian_with(keys[1], (M, 2, M // 2, N_GRP, M // N_GRP), (2 * M) ** -0.5, 0.1875, ((0, 48), (2, 4), (3, 4)), (3, 2, 4, 2.0))
    lat_points = draw_lat_points(jax.random.fold_in(keys[5], 71), 0)
    wave_slots = draw_wave_slots(jax.random.fold_in(keys[5], 71), 0)
    vertical = bell_draw(keys[4], (LEVELS, LEVELS), LEVELS ** -0.5, 2.0, (), jnp.float32)
    return {"fourier": fourier, "legendre": legendre, "lat_points": lat_points, "wave_slots": wave_slots, "vertical": vertical}


def per_slot(pieces):
    block, functions = pieces
    return jnp.einsum("cpr,pjr->pcj", block.astype(jnp.float32), functions.astype(jnp.float32), precision=lax.Precision.HIGHEST)


def reference(fourier, legendre, lat_points, wave_slots, vertical):
    cutoff = jnp.minimum(M - 1, (lat_points - 1) // 2)
    wave_ids = jnp.arange(M, dtype=jnp.int32)
    kept_mask = wave_ids[None, None, :] <= cutoff[:, :, None]
    masked = jnp.where(kept_mask, fourier, jnp.zeros((), fourier.dtype))
    ordered = jnp.take(masked, wave_slots, axis=6)
    level_ids = jnp.arange(LEVELS, dtype=jnp.int32)
    upper_part = level_ids[None, :] >= level_ids[:, None]
    integral = jnp.where(upper_part, vertical, jnp.zeros((), vertical.dtype))
    geopotential = jnp.einsum("lk,kcpgrs->lcpgrs", integral, ordered[2].astype(jnp.float32), precision=lax.Precision.HIGHEST).astype(jnp.bfloat16)
    fields = jnp.concatenate([ordered, geopotential[None]], axis=0)
    northern = fields[:, :, :, 0].astype(jnp.float32)
    southern = fields[:, :, :, 1].astype(jnp.float32)
    parity = jnp.stack([(northern + southern).astype(jnp.bfloat16), (northern - southern).astype(jnp.bfloat16)], axis=3)
    columns = parity.reshape((FIELDS + 1) * LEVELS * 2, 2, M, M)
    by_slot = jnp.transpose(columns, (3, 0, 1, 2))
    functions = legendre.reshape(M, 2, M // 2, M)
    raw = lax.map(per_slot, (by_slot, functions))
    raw = raw.reshape(M, 2, FIELDS + 1, LEVELS, 2, M // 2)
    half_ids = jnp.arange(M // 2, dtype=jnp.int32)
    parity_ids = jnp.arange(2, dtype=jnp.int32)
    total = wave_slots[:, None, None] + 2 * half_ids[None, None, :] + parity_ids[None, :, None]
    valid = (total <= M - 1)[:, :, None, None, None, :]
    return jnp.where(valid, raw, 0.0).astype(jnp.bfloat16)
```

```python
import functools

import jax
import jax.numpy as jnp
from jax import lax
from jax.experimental import pallas as pl
from jax.experimental.pallas import tpu as pltpu
from jax.sharding import PartitionSpec as P

MESH = pl.DeviceIdType.MESH
F32 = jnp.float32
BF16 = jnp.bfloat16

M = 1152
BANDS = 48
SLOTS = 24
LANES = 128
PACK = 32
KROWS = 144
JPAD = 40
COLS = 384


def third(x):
    return (x * 21846) >> 16


def iota(shape, dim):
    return lax.broadcasted_iota(jnp.int32, shape, dim)


def onehot(cond):
    return jnp.where(cond, 1.0, 0.0).astype(BF16)


def roll(x, shift):
    return pltpu.roll(x, shift % LANES, 1)


def dot(a, b):
    return jnp.dot(a, b, preferred_element_type=F32)


def dot_nt(a, b):
    return lax.dot_general(a, b, (((1,), (1,)), ((), ())), preferred_element_type=F32)


def swap_lanes(tiles, bits, lane):
    for bit, shift in bits:
        low = (lane & shift) == 0
        swapped = list(tiles)
        for a in range(len(tiles)):
            if a & bit:
                continue
            x, y = tiles[a], tiles[a | bit]
            swapped[a] = jnp.where(low, x, roll(y, shift))
            swapped[a | bit] = jnp.where(low, roll(x, -shift), y)
        tiles = swapped
    return tiles


def kernel(
    x_ref, leg_hbm, waves_ref, waves_smem, vert_smem, out_ref,
    xp, raw_leg, leg, colperm, expand, staged, band_send, band_recv, gathered, stat, prod, zrows,
    grp_send, grp_recv, m_sel, m_geo_hi, m_geo_lo, leg_tmp,
    leg_sem, bsend_sem, brecv_sem, ysend_sem, yrecv_sem, csend_sem, crecv_sem, fsend_sem, frecv_sem,
    gsend_sem, grecv_sem,
):
    band = lax.axis_index("band")
    lev = lax.axis_index("lev")
    grp = lax.axis_index("grp")
    core_peer = lev + 1 - 2 * (lev % 2)
    y_peer = (lev + 2) % 4
    far = (core_peer + 2) % 4

    barrier = pltpu.get_barrier_semaphore()

    def greet(d, carry):
        pl.semaphore_signal(barrier, inc=1, device_id={"band": (band + d) % BANDS}, device_id_type=MESH)
        return carry

    lax.fori_loop(1, BANDS, greet, 0)
    pl.semaphore_signal(barrier, inc=1, device_id={"lev": core_peer}, device_id_type=MESH)
    pl.semaphore_signal(barrier, inc=1, device_id={"lev": y_peer}, device_id_type=MESH)
    for d in range(1, 4):
        pl.semaphore_signal(barrier, inc=1, device_id={"grp": (grp + d) % 4}, device_id_type=MESH)

    leg_copy = pltpu.make_async_copy(leg_hbm, raw_leg, leg_sem)
    leg_copy.start()

    r = iota((256, 144), 0)
    col = iota((256, 144), 1)
    i, t = r >> 4, r & 15
    f = third(t)
    q = 2 * (t - 3 * f) + (i >> 3)
    src = ((f * 2 + ((i >> 1) & 1)) * 2 + (i & 1)) * 12 + q * 2 + ((i >> 2) & 1)
    place = onehot((t < 9) & (src == col))
    for n in range(0, M, 384):
        xp[:, n : n + 384] = dot(place, x_ref[:, n : n + 384]).astype(BF16)

    lane16 = iota((16, LANES), 1)
    wave_rows = iota((M, LANES), 0)

    def permute(tt, carry):
        for inner in range(3):
            at = pl.multiple_of((tt * 3 + inner) * LANES, LANES)
            table = onehot(wave_rows == waves_ref[:, pl.ds(at, LANES)])
            res = dot(xp[...], table)
            tiles = [res[16 * k : 16 * k + 16] for k in range(16)]
            tiles = swap_lanes(tiles, [(1, 8), (2, 16), (4, 32), (8, 64)], lane16)
            for g in range(16):
                staged[inner * 16 + g] = tiles[g]
        for b in range(16):
            a0, a1, a2 = staged[3 * b], staged[3 * b + 1], staged[3 * b + 2]
            extra = a0[8:16] + pltpu.roll(a1[8:16], 1, 0) + pltpu.roll(a2[8:16], 2, 0)
            packed = jnp.concatenate([a0[:8], a1[:8], a2[:8], extra], axis=0)
            band_send[tt * 16 + b] = packed.astype(BF16)
        return carry

    lax.fori_loop(0, 3, permute, 0)

    pl.semaphore_wait(barrier, BANDS - 1 + 2 + 3)

    def band_copy(d):
        to = (band + d) % BANDS
        return pltpu.make_async_remote_copy(
            src_ref=band_send.at[to], dst_ref=band_recv.at[band], send_sem=bsend_sem, recv_sem=brecv_sem,
            device_id={"band": to}, device_id_type=MESH,
        )

    def start_band(d, carry):
        band_copy(d).start()
        return carry

    lax.fori_loop(1, BANDS, start_band, 0)
    band_recv[band] = band_send[band]

    for k in range(3):
        for f in range(3):
            row = iota((48, 512), 0)
            col = iota((48, 512), 1)
            b = third(row)
            t = row - 3 * b + 3 * f
            expand[(k * 3 + f) * 48 : (k * 3 + f) * 48 + 48, :] = onehot(
                col == b * PACK + jnp.where(t < 8, 8 * k + t, 24 + k)
            )
    row = iota((288, 288), 0)
    col = iota((288, 288), 1)
    half = (col >= KROWS).astype(jnp.int32)
    rest = col - KROWS * half
    b = third(rest)
    colperm[...] = onehot(row == 6 * b + 2 * (rest - 3 * b) + half)

    row = iota((384, COLS), 0)
    col = iota((384, COLS), 1)
    block = third(row >> 4)
    inside = row - 48 * block
    tile, w = col >> 7, col & 127
    u = jnp.where(tile < 2, tile, w >> 6)
    fld = jnp.where(tile < 2, w >> 6, 2)
    lvl = ((w >> 1) & 3) * 2 + ((w >> 4) & 1)
    m_sel[...] = onehot(
        (block == u * 4 + (w & 1) * 2 + ((w >> 5) & 1)) & (inside == fld * 16 + lvl * 2 + ((w >> 3) & 1))
    )
    row = iota((128, LANES), 0)
    w = iota((128, LANES), 1)
    lvl = ((w >> 1) & 3) * 2 + ((w >> 4) & 1)
    same = ((row >> 4) == (w >> 6) * 4 + (w & 1) * 2 + ((w >> 5) & 1)) & ((row & 1) == ((w >> 3) & 1))
    pair = ((row >> 1) & 7) * 8 + lvl
    weight = jnp.zeros((128, LANES), F32)
    for a in range(8):
        for c in range(a, 8):
            weight = jnp.where(pair == a * 8 + c, vert_smem[a, c], weight)
    weight = jnp.where(same, weight, 0.0)
    m_geo_hi[...] = weight.astype(BF16)
    m_geo_lo[...] = (weight - weight.astype(BF16).astype(F32)).astype(BF16)

    leg_copy.wait()
    leg_tmp[288:296, :] = jnp.zeros((8, 288), F32)

    def prepare(s, carry):
        leg_tmp[:288, :] = dot(raw_leg[s].reshape(288, 288), colperm[...])
        for g in range(4):
            leg[s, 80 * g : 80 * g + 80, :] = jnp.concatenate(
                [leg_tmp[36 * g : 36 * g + JPAD, :], leg_tmp[144 + 36 * g : 144 + 36 * g + JPAD, :]], axis=0
            ).astype(BF16)
        return carry

    lax.fori_loop(0, SLOTS, prepare, 0)

    most = pl.ds(0, BANDS - 1)
    pltpu.make_async_remote_copy(
        src_ref=band_send.at[most], dst_ref=band_recv.at[most], send_sem=bsend_sem, recv_sem=brecv_sem,
        device_id={"band": band}, device_id_type=MESH,
    ).wait_recv()
    for c in range(3):
        rows = dot(expand[...], band_recv[16 * c : 16 * c + 16].reshape(512, LANES)).astype(BF16)
        for k in range(3):
            for f in range(3):
                n = (k * 3 + f) * 48
                gathered[lev, k, KROWS * f + 48 * c : KROWS * f + 48 * c + 48, :] = rows[n : n + 48]

    def lev_copy(k, owner, peer, send_sem, recv_sem):
        return pltpu.make_async_remote_copy(
            src_ref=gathered.at[owner, k], dst_ref=gathered.at[owner, k], send_sem=send_sem.at[k],
            recv_sem=recv_sem.at[k], device_id={"lev": peer}, device_id_type=MESH,
        )

    for k in range(3):
        lev_copy(k, lev, y_peer, ysend_sem, yrecv_sem).start()
        lev_copy(k, lev, core_peer, csend_sem, crecv_sem).start()

    lane = iota((16, LANES), 1)
    lane_j = iota((JPAD, LANES), 1)

    def grp_copy(k, d):
        to = (grp + d) % 4
        return pltpu.make_async_remote_copy(
            src_ref=grp_send.at[k, to], dst_ref=grp_recv.at[k, grp], send_sem=gsend_sem.at[k, d - 1],
            recv_sem=grecv_sem.at[k, d - 1], device_id={"grp": to}, device_id_type=MESH,
        )

    def finish(k):
        total = grp_send[k, grp].astype(F32)
        for d in range(1, 4):
            grp_copy(k, d).wait_recv()
            total = total + grp_recv[k, (grp + 4 - d) % 4].astype(F32)
        halves = 36 * (4 * lev + grp) + iota((64, JPAD), 1)
        for h in range(2):
            part = total[JPAD * h : JPAD * h + JPAD]
            hi = part.astype(BF16)
            lo = (part[:, 256:] - hi[:, 256:].astype(F32)).astype(BF16)
            plain = dot_nt(m_sel[...], hi)
            geo = dot_nt(m_geo_hi[...], hi[:, 256:]) + (
                dot_nt(m_geo_hi[...], lo) + dot_nt(m_geo_lo[...], hi[:, 256:])
            )
            for n in range(8):
                s, p = 8 * k + 4 * h + n // 2, n % 2
                wave = waves_smem[band * SLOTS + s]
                values = jnp.concatenate([plain[48 * n : 48 * n + 48], geo[16 * n : 16 * n + 16]], axis=0)
                values = jnp.where(wave + 2 * halves + p <= M - 1, values, 0.0).astype(BF16)
                out_ref[s, p] = values[:, :36]

    for k in range(3):
        lev_copy(k, y_peer, y_peer, ysend_sem, yrecv_sem).wait_recv()
        lev_copy(k, y_peer, core_peer, fsend_sem, frecv_sem).start()
        lev_copy(k, core_peer, core_peer, csend_sem, crecv_sem).wait_recv()
        lev_copy(k, far, core_peer, fsend_sem, frecv_sem).wait_recv()

        def blocks(rb, carry):
            per_field = []
            for f in range(3):
                at = pl.multiple_of(KROWS * f + 16 * rb, 16)
                tiles = [gathered[n, k, pl.ds(at, 16), :].astype(F32) for n in range(4)]
                per_field.append(swap_lanes(tiles, [(2, 4), (1, 2)], lane))
            first = pl.multiple_of(16 * rb, 16)
            second = pl.multiple_of(KROWS + 16 * rb, 16)
            for n in range(4):
                x0, x1, x2 = per_field[0][n], per_field[1][n], per_field[2][n]
                stat[n, pl.ds(first, 16), :LANES] = jnp.where(lane < 64, x0, roll(x1, 64)).astype(BF16)
                stat[n, pl.ds(first, 16), LANES:] = x2.astype(BF16)
                stat[n, pl.ds(second, 16), :LANES] = jnp.where(lane < 64, roll(x0, 64), x1).astype(BF16)
                stat[n, pl.ds(second, 16), LANES:] = roll(x2, 64).astype(BF16)
            return carry

        lax.fori_loop(0, 9, blocks, 0)

        for n in range(4):
            for s in range(2):
                prod[s] = dot(leg[8 * k + 2 * n + s], stat[n])
            for g in range(4):
                for tile in range(2):
                    lanes = slice(LANES * tile, LANES * tile + LANES)
                    even = (lane_j & 1) == 0
                    north = (lane_j & 32) == 0
                    p0 = jnp.where(even, prod[0, 80 * g : 80 * g + 40, lanes], prod[1, 80 * g : 80 * g + 40, lanes])
                    p1 = jnp.where(even, prod[0, 80 * g + 40 : 80 * g + 80, lanes], prod[1, 80 * g + 40 : 80 * g + 80, lanes])
                    zrows[n, 40 * g : 40 * g + 40, lanes] = jnp.where(north, p0 + roll(p0, -32), roll(p1, 32) - p1)
        for g in range(4):
            rows = slice(40 * g, 40 * g + 40)
            halves = []
            for h in range(2):
                last = jnp.where(lane_j < 64, zrows[2 * h, rows, LANES:], roll(zrows[2 * h + 1, rows, LANES:], 64))
                halves.append(jnp.concatenate([zrows[2 * h, rows, :LANES], zrows[2 * h + 1, rows, :LANES], last], axis=1))
            grp_send[k, g] = jnp.concatenate(halves, axis=0).astype(BF16)
        for d in (2, 1, 3):
            grp_copy(k, d).start()
        if k:
            finish(k - 1)
    finish(2)

    pltpu.make_async_remote_copy(
        src_ref=band_send.at[most], dst_ref=band_recv.at[most], send_sem=bsend_sem, recv_sem=brecv_sem,
        device_id={"band": band}, device_id_type=MESH,
    ).wait_send()
    for k in range(3):
        lev_copy(k, lev, y_peer, ysend_sem, yrecv_sem).wait_send()
        lev_copy(k, lev, core_peer, csend_sem, crecv_sem).wait_send()
        lev_copy(k, y_peer, core_peer, fsend_sem, frecv_sem).wait_send()
        for d in range(1, 4):
            grp_copy(k, d).wait_send()


def body(fourier, legendre, lat_points, wave_slots, vertical):
    cutoff = jnp.minimum(M - 1, (lat_points - 1) // 2)[0]
    moved = jnp.transpose(fourier[:, :, :, :, 0], (0, 1, 2, 4, 3, 5))
    kept = iota((1, 1, 1, 6, 1, M), 5) <= cutoff[None, None, None, :, None, None]
    rows = jnp.where(kept, moved, jnp.zeros((), moved.dtype)).reshape(144, M)
    vmem = pl.BlockSpec(memory_space=pltpu.VMEM)
    smem = pl.BlockSpec(memory_space=pltpu.SMEM)
    dma = pltpu.SemaphoreType.DMA
    out = pl.pallas_call(
        kernel,
        out_shape=jax.ShapeDtypeStruct((SLOTS, 2, 64, 36), BF16),
        in_specs=[vmem, pl.BlockSpec(memory_space=pl.ANY), vmem, smem, smem],
        out_specs=vmem,
        scratch_shapes=[
            pltpu.VMEM((256, M), BF16),
            pltpu.VMEM((SLOTS, 2, KROWS, 288), BF16),
            pltpu.VMEM((SLOTS, 320, 288), BF16),
            pltpu.VMEM((288, 288), BF16),
            pltpu.VMEM((432, 512), BF16),
            pltpu.VMEM((48, 16, LANES), F32),
            pltpu.VMEM((BANDS, PACK, LANES), BF16),
            pltpu.VMEM((BANDS, PACK, LANES), BF16),
            pltpu.VMEM((4, 3, 432, LANES), BF16),
            pltpu.VMEM((4, 288, 256), BF16),
            pltpu.VMEM((2, 320, 256), F32),
            pltpu.VMEM((4, 160, 256), F32),
            pltpu.VMEM((3, 4, 80, COLS), BF16),
            pltpu.VMEM((3, 4, 80, COLS), BF16),
            pltpu.VMEM((384, COLS), BF16),
            pltpu.VMEM((128, LANES), BF16),
            pltpu.VMEM((128, LANES), BF16),
            pltpu.VMEM((296, 288), F32),
            dma, dma, dma,
            dma((3,)), dma((3,)), dma((3,)), dma((3,)), dma((3,)), dma((3,)),
            dma((3, 3)), dma((3, 3)),
        ],
        compiler_params=pltpu.CompilerParams(
            collective_id=0, has_side_effects=True, vmem_limit_bytes=48 * 1024 * 1024
        ),
        cost_estimate=pl.CostEstimate(flops=10**9, bytes_accessed=10**7, transcendentals=0),
    )(rows, legendre.reshape(SLOTS, 2, KROWS, 288), wave_slots.reshape(1, M), wave_slots, vertical)
    return out.reshape(SLOTS, 2, 4, 8, 2, 36)


def solution(mesh):
    placed = (
        P(None, "lev", None, None, "grp", "band", None),
        P("band", None, "lev", "grp", None),
        P("grp", "band"),
        P(),
        P(),
    )
    return jax.shard_map(
        body,
        mesh=mesh,
        in_specs=placed,
        out_specs=P("band", None, None, None, None, ("lev", "grp")),
        check_vma=False,
    )
```

```python
import functools

import jax
import jax.numpy as jnp
from jax import lax
from jax.experimental import pallas as pl
from jax.experimental.pallas import tpu as pltpu
from jax.sharding import PartitionSpec as P

MESH = pl.DeviceIdType.MESH
F32 = jnp.float32
BF16 = jnp.bfloat16

M = 1152
BANDS = 48
SLOTS = 24
LANES = 128
PACK = 32
KROWS = 144
JPAD = 40
COLS = 384


def third(x):
    return (x * 21846) >> 16


def iota(shape, dim):
    return lax.broadcasted_iota(jnp.int32, shape, dim)


def onehot(cond):
    return jnp.where(cond, 1.0, 0.0).astype(BF16)


def roll(x, shift):
    return pltpu.roll(x, shift % LANES, 1)


def dot(a, b):
    return jnp.dot(a, b, preferred_element_type=F32)


def dot_nt(a, b):
    return lax.dot_general(a, b, (((1,), (1,)), ((), ())), preferred_element_type=F32)


def swap_lanes(tiles, bits, lane):
    for bit, shift in bits:
        low = (lane & shift) == 0
        swapped = list(tiles)
        for a in range(len(tiles)):
            if a & bit:
                continue
            x, y = tiles[a], tiles[a | bit]
            swapped[a] = jnp.where(low, x, roll(y, shift))
            swapped[a | bit] = jnp.where(low, roll(x, -shift), y)
        tiles = swapped
    return tiles


def nearest(p):
    odd = p % 2
    return odd * ((p + 1) // 2) - (1 - odd) * (p // 2)


def kernel(
    x_hbm, lat_hbm, waves_hbm, vert_hbm, leg_hbm, out_ref,
    x_ref, lat_ref, waves_ref, vert_ref, xp, raw_leg, leg, colperm, expand, band_send, band_recv, gathered, stat, prod,
    grp_send, grp_recv, m_sel, m_geo_hi, m_geo_lo, leg_tmp, wave_col,
    in_sem, leg_sem, bsend_sem, brecv_sem, ysend_sem, yrecv_sem, csend_sem, crecv_sem, fsend_sem, frecv_sem,
    gsend_sem, grecv_sem,
):
    band = lax.axis_index("band")
    lev = lax.axis_index("lev")
    grp = lax.axis_index("grp")
    z, yh = band // 4, band % 4
    core_peer = lev + 1 - 2 * (lev % 2)
    y_peer = (lev + 2) % 4
    far = (core_peer + 2) % 4

    x_copy = pltpu.make_async_copy(x_hbm, x_ref, in_sem.at[0])
    lat_copy = pltpu.make_async_copy(lat_hbm, lat_ref, in_sem.at[1])
    waves_copy = pltpu.make_async_copy(waves_hbm, waves_ref, in_sem.at[2])
    vert_copy = pltpu.make_async_copy(vert_hbm, vert_ref, in_sem.at[3])
    for copy in (x_copy, lat_copy, waves_copy, vert_copy):
        copy.start()

    barrier = pltpu.get_barrier_semaphore()

    def greet(d, carry):
        pl.semaphore_signal(barrier, inc=1, device_id={"band": (band + d) % BANDS}, device_id_type=MESH)
        return carry

    lax.fori_loop(1, BANDS, greet, 0)
    pl.semaphore_signal(barrier, inc=1, device_id={"lev": core_peer}, device_id_type=MESH)
    pl.semaphore_signal(barrier, inc=1, device_id={"lev": y_peer}, device_id_type=MESH)
    for d in range(1, 4):
        pl.semaphore_signal(barrier, inc=1, device_id={"grp": (grp + d) % 4}, device_id_type=MESH)

    leg_copy = pltpu.make_async_copy(leg_hbm, raw_leg, leg_sem)
    leg_copy.start()

    r = iota((256, 144), 0)
    col = iota((256, 144), 1)
    i, t = r >> 4, r & 15
    f = third(t)
    q = 2 * (t - 3 * f) + (i >> 3)
    src = ((f * 2 + ((i >> 1) & 1)) * 2 + (i & 1)) * 12 + q * 2 + ((i >> 2) & 1)
    place = onehot((t < 9) & (src == col))
    row = iota((384, 384), 0)
    col = iota((384, 384), 1)
    turned = 2 * (((col >> 1) & 3) + 4 - lev & 3) + (col & 1)
    regroup = onehot(row == ((col >> 3) & 15) * 24 + (col >> 7) * 8 + turned)
    pair = iota((144, 384), 0) >> 1
    pair = pair - 6 * third(pair >> 1)
    lat_copy.wait()
    cutoff = jnp.zeros((144, 384), jnp.int32)
    for q in range(6):
        cutoff = jnp.where(pair == q, (lat_ref[0:1, q : q + 1] - 1) >> 1, cutoff)
    x_copy.wait()
    for n in range(0, M, 384):
        lines = x_ref[:, :, n : n + 384].reshape(144, 384)
        kept = jnp.where(iota((144, 384), 1) + n <= cutoff, lines, jnp.zeros((), BF16))
        xp[:, n : n + 384] = dot(place, kept).astype(BF16)

    lane = iota((16, LANES), 1)
    wave_rows = iota((M, LANES), 0)

    def permute(tt, carry):
        parts = []
        line = jnp.concatenate([waves_ref[pl.ds(tt * 3 + n, 1), :] for n in range(3)], axis=1)
        line = jnp.broadcast_to(line, (16, 384))
        digits = jnp.where(iota((16, 384), 0) == 0, line >> 5, line & 31).astype(F32).astype(BF16)
        digits = dot(digits, regroup)
        waves = (32.0 * digits[0:1] + digits[1:2]).astype(jnp.int32)
        for k in range(3):
            res = dot(xp[...], onehot(wave_rows == waves[:, LANES * k : LANES * k + LANES]))
            tiles = [None] * 16
            for n in range(16):
                if n & 4 == 0:
                    north, south = res[16 * n : 16 * n + 16], res[16 * n + 64 : 16 * n + 80]
                    tiles[n], tiles[n | 4] = north + south, north - south
            parts.append(tiles)
        upper = [jnp.concatenate([parts[0][n][:8], parts[1][n][:8]], axis=0).astype(BF16) for n in range(16)]
        lower = []
        for n in range(16):
            extra = parts[0][n][8:] + pltpu.roll(parts[1][n][8:], 1, 0) + pltpu.roll(parts[2][n][8:], 2, 0)
            lower.append(jnp.concatenate([parts[2][n][:8], extra], axis=0).astype(BF16))
        for h, tiles in enumerate((upper, lower)):
            tiles = swap_lanes(tiles, [(1, 8), (2, 16), (4, 32), (8, 64)], lane)
            for g in range(16):
                band_send[tt * 16 + g, 16 * h : 16 * h + 16, :] = tiles[g]
        return carry

    waves_copy.wait()
    lax.fori_loop(0, 3, permute, 0)

    pl.semaphore_wait(barrier, BANDS - 1 + 2 + 3)

    def start_band(c, first):
        def start(t, carry):
            p = 4 * c + t % 4
            to = ((z - nearest(p) + 12) % 12) * 4 + (yh + t // 4) % 4
            pltpu.make_async_remote_copy(
                src_ref=band_send.at[to], dst_ref=band_recv.at[p * 4 + yh], send_sem=bsend_sem,
                recv_sem=brecv_sem.at[c], device_id={"band": to}, device_id_type=MESH,
            ).start()
            return carry

        lax.fori_loop(first, 16, start, 0)

    for c in range(3):
        start_band(c, 1 if c == 0 else 0)
    band_recv[yh] = band_send[band]

    def band_messages(start, count, c):
        part = pl.ds(start, count)
        return pltpu.make_async_remote_copy(
            src_ref=band_send.at[part], dst_ref=band_recv.at[part], send_sem=bsend_sem, recv_sem=brecv_sem.at[c],
            device_id={"band": band}, device_id_type=MESH,
        )

    for k in range(3):
        for f in range(3):
            row = iota((48, 512), 0)
            col = iota((48, 512), 1)
            b = third(row)
            t = row - 3 * b + 3 * f
            expand[(k * 3 + f) * 48 : (k * 3 + f) * 48 + 48, :] = onehot(
                col == b * PACK + jnp.where(t < 8, 8 * k + t, 24 + k)
            )
    row = iota((288, 288), 0)
    col = iota((288, 288), 1)
    half = (col >= KROWS).astype(jnp.int32)
    rest = col - KROWS * half
    b = third(rest)
    p = b >> 2
    away = jnp.where((p & 1) == 1, (p + 1) >> 1, -(p >> 1)) + z
    away = jnp.where(away < 0, away + 12, jnp.where(away >= 12, away - 12, away))
    colperm[...] = onehot(row == 6 * (away * 4 + (b & 3)) + 2 * (rest - 3 * b) + half)

    leg_copy.wait()
    leg_tmp[288:296, :] = jnp.zeros((8, 288), F32)

    def prepare(s, carry):
        leg_tmp[:288, :] = dot(raw_leg[s].reshape(288, 288), colperm[...])
        for g in range(4):
            leg[s, 80 * g : 80 * g + 80, :] = jnp.concatenate(
                [leg_tmp[36 * g : 36 * g + JPAD, :], leg_tmp[144 + 36 * g : 144 + 36 * g + JPAD, :]], axis=0
            ).astype(BF16)
        return carry

    def lev_copy(n, owner, peer, send_sem, recv_sem):
        part = gathered.at[owner, n] if n < 2 else gathered.at[owner, 2, pl.ds(KROWS * (n - 2), KROWS)]
        return pltpu.make_async_remote_copy(
            src_ref=part, dst_ref=part, send_sem=send_sem.at[n], recv_sem=recv_sem.at[n],
            device_id={"lev": peer}, device_id_type=MESH,
        )

    def forward(n):
        lev_copy(n, y_peer, y_peer, ysend_sem, yrecv_sem).wait_recv()
        lev_copy(n, y_peer, core_peer, fsend_sem, frecv_sem).start()

    def send_levels(n):
        lev_copy(n, lev, y_peer, ysend_sem, yrecv_sem).start()
        lev_copy(n, lev, core_peer, csend_sem, crecv_sem).start()

    def levels_here(n):
        lev_copy(n, core_peer, core_peer, csend_sem, crecv_sem).wait_recv()
        lev_copy(n, far, core_peer, fsend_sem, frecv_sem).wait_recv()

    lane48 = iota((48, LANES), 1)

    def sixteen_bands(c):
        band_messages(0, 15 if c == 0 else 16, c).wait_recv()
        rows = dot(expand[...], band_recv[16 * c : 16 * c + 16].reshape(512, LANES)).astype(BF16)
        for k in range(3):
            at = k * KROWS
            x0, x1, x2 = rows[at : at + 48], rows[at + 48 : at + 96], rows[at + 96 : at + 144]
            gathered[lev, c, at : at + 48, :] = jnp.where(lane48 < 64, x0, roll(x1, 64))
            gathered[lev, c, at + 48 : at + 96, :] = jnp.where(lane48 < 64, roll(x0, 64), x1)
            gathered[lev, c, at + 96 : at + 144, :] = x2
            if c == 2:
                send_levels(2 + k)

    lax.fori_loop(0, 8, prepare, 0)
    vert_copy.wait()

    for h in range(2):
        row = iota((384, COLS), 0)
        col = iota((384, COLS), 1)
        block = third(row >> 4)
        inside = row - 48 * block
        tile, w = col >> 7, col & 127
        u = jnp.where(tile < 2, tile, w >> 6)
        fld = jnp.where(tile < 2, w >> 6, 2)
        lvl = ((((w >> 1) & 3) - 2 * h - u) & 3) * 2 + ((w >> 4) & 1)
        m_sel[h] = onehot(
            (block == u * 4 + (w & 1) * 2 + ((w >> 5) & 1)) & (inside == fld * 16 + lvl * 2 + ((w >> 3) & 1))
        )
        row = iota((128, LANES), 0)
        w = iota((128, LANES), 1)
        lvl = ((((w >> 1) & 3) - 2 * h - (w >> 6)) & 3) * 2 + ((w >> 4) & 1)
        same = ((row >> 4) == (w >> 6) * 4 + (w & 1) * 2 + ((w >> 5) & 1)) & ((row & 1) == ((w >> 3) & 1))
        pair = ((row >> 1) & 7) * 8 + lvl
        weight = jnp.zeros((128, LANES), F32)
        for a in range(8):
            for c in range(a, 8):
                weight = jnp.where(pair == a * 8 + c, vert_ref[a : a + 1, c : c + 1], weight)
        weight = jnp.where(same, weight, 0.0)
        m_geo_hi[h] = weight.astype(BF16)
        m_geo_lo[h] = (weight - weight.astype(BF16).astype(F32)).astype(BF16)
    mine = band * SLOTS + iota((SLOTS, LANES), 0)
    owned = jnp.zeros((SLOTS, LANES), F32)
    for n in range(9):
        here = iota((SLOTS, LANES), 1) + LANES * n == mine
        owned = owned + jnp.where(here, waves_ref[n : n + 1, :].astype(F32), 0.0)
    owned = jnp.sum(owned, axis=1, keepdims=True)
    wave_col[...] = jnp.broadcast_to(owned, (SLOTS, LANES)).astype(jnp.int32)

    sixteen_bands(0)
    send_levels(0)
    lax.fori_loop(8, 16, prepare, 0)
    sixteen_bands(1)
    send_levels(1)
    forward(0)
    lax.fori_loop(16, 24, prepare, 0)
    sixteen_bands(2)
    forward(1)
    for n in range(2):
        levels_here(n)

    lane_j = iota((JPAD, LANES), 1)

    def grp_copy(k, d):
        to = (grp + d) % 4
        return pltpu.make_async_remote_copy(
            src_ref=grp_send.at[k, to], dst_ref=grp_recv.at[k, grp], send_sem=gsend_sem.at[k, d - 1],
            recv_sem=grecv_sem.at[k, d - 1], device_id={"grp": to}, device_id_type=MESH,
        )

    def finish(k):
        total = grp_send[k, grp].astype(F32)
        for d in range(1, 4):
            grp_copy(k, d).wait_recv()
            total = total + grp_recv[k, (grp + 4 - d) % 4].astype(F32)
        halves = 36 * (4 * lev + grp) + iota((64, JPAD), 1)
        for h in range(2):
            part = total[JPAD * h : JPAD * h + JPAD]
            hi = part.astype(BF16)
            lo = (part[:, 256:] - hi[:, 256:].astype(F32)).astype(BF16)
            plain = dot_nt(m_sel[h], hi)
            geo = dot_nt(m_geo_hi[h], hi[:, 256:]) + (
                dot_nt(m_geo_hi[h], lo) + dot_nt(m_geo_lo[h], hi[:, 256:])
            )
            for n in range(8):
                s, p = 8 * k + 4 * h + n // 2, n % 2
                values = jnp.concatenate([plain[48 * n : 48 * n + 48], geo[16 * n : 16 * n + 16]], axis=0)
                valid = wave_col[s : s + 1, :JPAD] + 2 * halves + p <= M - 1
                out_ref[s, p] = jnp.where(valid, values, 0.0).astype(BF16)[:, :36]

    group = (lane >> 1) & 3
    forward(2)
    for k in range(3):
        levels_here(2 + k)

        def blocks(rb, carry):
            c, o = rb // 3, rb % 3
            first = pl.multiple_of(16 * rb, 16)
            second = pl.multiple_of(KROWS + 16 * rb, 16)
            per_kind = []
            for f in range(3):
                at = pl.multiple_of(k * KROWS + 48 * f + 16 * o, 16)
                per_kind.append([gathered[n, c, pl.ds(at, 16), :] for n in range(4)])
            for n in range(4):
                picked = []
                for tiles in per_kind:
                    x = tiles[(3 - n) % 4]
                    for a in range(3):
                        x = jnp.where(group == a, tiles[(a - n) % 4], x)
                    picked.append(x)
                stat[n, pl.ds(first, 16), :LANES] = picked[0]
                stat[n, pl.ds(second, 16), :LANES] = picked[1]
                turned = roll(picked[2], 64)
                stat[n, pl.ds(first, 16), LANES:] = turned if n % 2 else picked[2]
                stat[n, pl.ds(second, 16), LANES:] = picked[2] if n % 2 else turned
            return carry

        lax.fori_loop(0, 9, blocks, 0)
        if k < 2:
            forward(3 + k)

        for n in range(8):
            prod[n] = dot(leg[8 * k + n], stat[n // 2])
        even = (lane_j & 1) == 0
        north = (lane_j & 32) == 0
        for g in range(4):
            halves = []
            for h in range(2):
                cols = []
                for n in (2 * h, 2 * h + 1):
                    for tile in range(2):
                        lanes = slice(LANES * tile, LANES * tile + LANES)
                        p0, p1 = slice(80 * g, 80 * g + 40), slice(80 * g + 40, 80 * g + 80)
                        cols.append(
                            jnp.where(
                                north,
                                jnp.where(even, prod[2 * n, p0, lanes], prod[2 * n + 1, p0, lanes]),
                                jnp.where(even, prod[2 * n, p1, lanes], prod[2 * n + 1, p1, lanes]),
                            )
                        )
                halves.append(jnp.concatenate([cols[0], cols[2], jnp.where(lane_j < 64, cols[1], cols[3])], axis=1))
            grp_send[k, g] = jnp.concatenate(halves, axis=0).astype(BF16)
        for d in (2, 1, 3):
            grp_copy(k, d).start()
        if k:
            finish(k - 1)
    finish(2)

    band_messages(0, BANDS - 1, 0).wait_send()
    for n in range(5):
        lev_copy(n, lev, y_peer, ysend_sem, yrecv_sem).wait_send()
        lev_copy(n, lev, core_peer, csend_sem, crecv_sem).wait_send()
        lev_copy(n, y_peer, core_peer, fsend_sem, frecv_sem).wait_send()
    for k in range(3):
        for d in range(1, 4):
            grp_copy(k, d).wait_send()


def body(fourier, legendre, lat_points, wave_slots, vertical):
    moved = jnp.transpose(fourier[:, :, :, :, 0], (0, 1, 2, 4, 3, 5)).reshape(72, 2, M)
    waves = wave_slots.reshape(9, LANES)
    hbm = pl.BlockSpec(memory_space=pltpu.HBM)
    vmem = pl.BlockSpec(memory_space=pltpu.VMEM)
    dma = pltpu.SemaphoreType.DMA
    out = pl.pallas_call(
        kernel,
        out_shape=jax.ShapeDtypeStruct((SLOTS, 2, 64, 36), BF16),
        in_specs=[hbm] * 5,
        out_specs=vmem,
        scratch_shapes=[
            pltpu.VMEM((72, 2, M), BF16),
            pltpu.VMEM((1, 6), jnp.int32),
            pltpu.VMEM((9, LANES), jnp.int32),
            pltpu.VMEM((8, 8), F32),
            pltpu.VMEM((256, M), BF16),
            pltpu.VMEM((SLOTS, 2, KROWS, 288), BF16),
            pltpu.VMEM((SLOTS, 320, 288), BF16),
            pltpu.VMEM((288, 288), BF16),
            pltpu.VMEM((432, 512), BF16),
            pltpu.VMEM((BANDS, PACK, LANES), BF16),
            pltpu.VMEM((BANDS, PACK, LANES), BF16),
            pltpu.VMEM((4, 3, 432, LANES), BF16),
            pltpu.VMEM((4, 288, 256), BF16),
            pltpu.VMEM((8, 320, 256), F32),
            pltpu.VMEM((3, 4, 80, COLS), BF16),
            pltpu.VMEM((3, 4, 80, COLS), BF16),
            pltpu.VMEM((2, 384, COLS), BF16),
            pltpu.VMEM((2, 128, LANES), BF16),
            pltpu.VMEM((2, 128, LANES), BF16),
            pltpu.VMEM((296, 288), F32),
            pltpu.VMEM((SLOTS, LANES), jnp.int32),
            dma((4,)), dma, dma, dma((3,)),
            dma((5,)), dma((5,)), dma((5,)), dma((5,)), dma((5,)), dma((5,)),
            dma((3, 3)), dma((3, 3)),
        ],
        compiler_params=pltpu.CompilerParams(
            collective_id=0, has_side_effects=True, vmem_limit_bytes=48 * 1024 * 1024
        ),
        cost_estimate=pl.CostEstimate(flops=10**9, bytes_accessed=10**7, transcendentals=0),
    )(moved, lat_points, waves, vertical, legendre.reshape(SLOTS, 2, KROWS, 288))
    return out.reshape(SLOTS, 2, 4, 8, 2, 36)


def solution(mesh):
    placed = (
        P(None, "lev", None, None, "grp", "band", None),
        P("band", None, "lev", "grp", None),
        P("grp", "band"),
        P(),
        P(),
    )
    return jax.shard_map(
        body,
        mesh=mesh,
        in_specs=placed,
        out_specs=P("band", None, None, None, None, ("lev", "grp")),
        check_vma=False,
    )
```

```python
import functools

import jax
import jax.numpy as jnp
from jax import lax
from jax.experimental import pallas as pl
from jax.experimental.pallas import tpu as pltpu
from jax.sharding import PartitionSpec as P

MESH = pl.DeviceIdType.MESH
F32 = jnp.float32
BF16 = jnp.bfloat16

M = 1152
BANDS = 48
SLOTS = 24
LANES = 128
PACK = 32
KROWS = 144
JPAD = 40
COLS = 384


def third(x):
    return (x * 21846) >> 16


def iota(shape, dim):
    return lax.broadcasted_iota(jnp.int32, shape, dim)


def onehot(cond):
    return jnp.where(cond, 1.0, 0.0).astype(BF16)


def roll(x, shift):
    return pltpu.roll(x, shift % LANES, 1)


def dot(a, b):
    return jnp.dot(a, b, preferred_element_type=F32)


def dot_nt(a, b):
    return lax.dot_general(a, b, (((1,), (1,)), ((), ())), preferred_element_type=F32)


def swap_lanes(tiles, bits, lane):
    for bit, shift in bits:
        low = (lane & shift) == 0
        swapped = list(tiles)
        for a in range(len(tiles)):
            if a & bit:
                continue
            x, y = tiles[a], tiles[a | bit]
            swapped[a] = jnp.where(low, x, roll(y, shift))
            swapped[a | bit] = jnp.where(low, roll(x, -shift), y)
        tiles = swapped
    return tiles


def nearest(p):
    odd = p % 2
    return odd * ((p + 1) // 2) - (1 - odd) * (p // 2)


def kernel(
    x_hbm, lat_hbm, waves_hbm, vert_hbm, leg_hbm, out_ref,
    x_ref, lat_ref, waves_ref, vert_ref, xp, raw_leg, leg, colperm, expand, band_send, band_recv, gathered, stat, prod,
    grp_send, grp_recv, m_sel, m_geo_hi, m_geo_lo, leg_tmp, wave_col,
    in_sem, leg_sem, bsend_sem, brecv_sem, ysend_sem, yrecv_sem, csend_sem, crecv_sem, fsend_sem, frecv_sem,
    gsend_sem, grecv_sem,
):
    band = lax.axis_index("band")
    lev = lax.axis_index("lev")
    grp = lax.axis_index("grp")
    z, yh = band // 4, band % 4
    core_peer = lev + 1 - 2 * (lev % 2)
    y_peer = (lev + 2) % 4
    far = (core_peer + 2) % 4

    x_copy = pltpu.make_async_copy(x_hbm, x_ref, in_sem.at[0])
    lat_copy = pltpu.make_async_copy(lat_hbm, lat_ref, in_sem.at[1])
    waves_copy = pltpu.make_async_copy(waves_hbm, waves_ref, in_sem.at[2])
    vert_copy = pltpu.make_async_copy(vert_hbm, vert_ref, in_sem.at[3])
    for copy in (x_copy, lat_copy, waves_copy, vert_copy):
        copy.start()

    barrier = pltpu.get_barrier_semaphore()

    def greet(d, carry):
        pl.semaphore_signal(barrier, inc=1, device_id={"band": (band + d) % BANDS}, device_id_type=MESH)
        return carry

    lax.fori_loop(1, BANDS, greet, 0)
    pl.semaphore_signal(barrier, inc=1, device_id={"lev": core_peer}, device_id_type=MESH)
    pl.semaphore_signal(barrier, inc=1, device_id={"lev": y_peer}, device_id_type=MESH)
    for d in range(1, 4):
        pl.semaphore_signal(barrier, inc=1, device_id={"grp": (grp + d) % 4}, device_id_type=MESH)

    leg_copy = pltpu.make_async_copy(leg_hbm, raw_leg, leg_sem)
    leg_copy.start()

    r = iota((256, 144), 0)
    col = iota((256, 144), 1)
    i, t = r >> 4, r & 15
    f = third(t)
    q = 2 * (t - 3 * f) + (i >> 3)
    src = ((f * 2 + ((i >> 1) & 1)) * 2 + (i & 1)) * 12 + q * 2 + ((i >> 2) & 1)
    place = onehot((t < 9) & (src == col))
    row = iota((384, 384), 0)
    col = iota((384, 384), 1)
    turned = 2 * (((col >> 1) & 3) + 4 - lev & 3) + (col & 1)
    regroup = onehot(row == ((col >> 3) & 15) * 24 + (col >> 7) * 8 + turned)
    pair = iota((144, 384), 0) >> 1
    pair = pair - 6 * third(pair >> 1)
    lat_copy.wait()
    cutoff = jnp.zeros((144, 384), jnp.int32)
    for q in range(6):
        cutoff = jnp.where(pair == q, (lat_ref[0:1, q : q + 1] - 1) >> 1, cutoff)
    x_copy.wait()
    for n in range(0, M, 384):
        lines = x_ref[:, :, n : n + 384].reshape(144, 384)
        kept = jnp.where(iota((144, 384), 1) + n <= cutoff, lines, jnp.zeros((), BF16))
        xp[:, n : n + 384] = dot(place, kept).astype(BF16)

    lane = iota((16, LANES), 1)
    wave_rows = iota((M, LANES), 0)

    def permute(tt, carry):
        parts = []
        line = jnp.concatenate([waves_ref[pl.ds(tt * 3 + n, 1), :] for n in range(3)], axis=1)
        line = jnp.broadcast_to(line, (16, 384))
        digits = jnp.where(iota((16, 384), 0) == 0, line >> 5, line & 31).astype(F32).astype(BF16)
        digits = dot(digits, regroup)
        waves = (32.0 * digits[0:1] + digits[1:2]).astype(jnp.int32)
        for k in range(3):
            res = dot(xp[...], onehot(wave_rows == waves[:, LANES * k : LANES * k + LANES]))
            tiles = [None] * 16
            for n in range(16):
                if n & 4 == 0:
                    north, south = res[16 * n : 16 * n + 16], res[16 * n + 64 : 16 * n + 80]
                    tiles[n], tiles[n | 4] = north + south, north - south
            parts.append(tiles)
        upper = [jnp.concatenate([parts[0][n][:8], parts[1][n][:8]], axis=0).astype(BF16) for n in range(16)]
        lower = []
        for n in range(16):
            extra = parts[0][n][8:] + pltpu.roll(parts[1][n][8:], 1, 0) + pltpu.roll(parts[2][n][8:], 2, 0)
            lower.append(jnp.concatenate([parts[2][n][:8], extra], axis=0).astype(BF16))
        for h, tiles in enumerate((upper, lower)):
            tiles = swap_lanes(tiles, [(1, 8), (2, 16), (4, 32), (8, 64)], lane)
            for g in range(16):
                band_send[tt * 16 + g, 16 * h : 16 * h + 16, :] = tiles[g]
        return carry

    waves_copy.wait()
    lax.fori_loop(0, 3, permute, 0)

    pl.semaphore_wait(barrier, BANDS - 1 + 2 + 3)

    def start_band(c, first):
        def start(t, carry):
            p = 4 * c + t % 4
            to = ((z - nearest(p) + 12) % 12) * 4 + (yh + t // 4) % 4
            pltpu.make_async_remote_copy(
                src_ref=band_send.at[to], dst_ref=band_recv.at[p * 4 + yh], send_sem=bsend_sem,
                recv_sem=brecv_sem.at[c], device_id={"band": to}, device_id_type=MESH,
            ).start()
            return carry

        lax.fori_loop(first, 16, start, 0)

    for c in range(3):
        start_band(c, 1 if c == 0 else 0)
    band_recv[yh] = band_send[band]

    def band_messages(start, count, c):
        part = pl.ds(start, count)
        return pltpu.make_async_remote_copy(
            src_ref=band_send.at[part], dst_ref=band_recv.at[part], send_sem=bsend_sem, recv_sem=brecv_sem.at[c],
            device_id={"band": band}, device_id_type=MESH,
        )

    for k in range(3):
        for f in range(3):
            row = iota((48, 512), 0)
            col = iota((48, 512), 1)
            b = third(row)
            t = row - 3 * b + 3 * f
            expand[(k * 3 + f) * 48 : (k * 3 + f) * 48 + 48, :] = onehot(
                col == b * PACK + jnp.where(t < 8, 8 * k + t, 24 + k)
            )
    row = iota((288, 288), 0)
    col = iota((288, 288), 1)
    half = (col >= KROWS).astype(jnp.int32)
    rest = col - KROWS * half
    b = third(rest)
    p = b >> 2
    away = jnp.where((p & 1) == 1, (p + 1) >> 1, -(p >> 1)) + z
    away = jnp.where(away < 0, away + 12, jnp.where(away >= 12, away - 12, away))
    colperm[...] = onehot(row == 6 * (away * 4 + (b & 3)) + 2 * (rest - 3 * b) + half)

    leg_copy.wait()
    leg_tmp[288:296, :] = jnp.zeros((8, 288), F32)

    def prepare(s, carry):
        leg_tmp[:288, :] = dot(raw_leg[s].reshape(288, 288), colperm[...])
        for g in range(4):
            leg[s, 80 * g : 80 * g + 80, :] = jnp.concatenate(
                [leg_tmp[36 * g : 36 * g + JPAD, :], leg_tmp[144 + 36 * g : 144 + 36 * g + JPAD, :]], axis=0
            ).astype(BF16)
        return carry

    def lev_copy(n, owner, peer, send_sem, recv_sem):
        part = gathered.at[owner, n] if n < 2 else gathered.at[owner, 2, pl.ds(KROWS * (n - 2), KROWS)]
        return pltpu.make_async_remote_copy(
            src_ref=part, dst_ref=part, send_sem=send_sem.at[n], recv_sem=recv_sem.at[n],
            device_id={"lev": peer}, device_id_type=MESH,
        )

    def forward(n):
        lev_copy(n, y_peer, y_peer, ysend_sem, yrecv_sem).wait_recv()
        lev_copy(n, y_peer, core_peer, fsend_sem, frecv_sem).start()

    def send_levels(n):
        lev_copy(n, lev, y_peer, ysend_sem, yrecv_sem).start()
        lev_copy(n, lev, core_peer, csend_sem, crecv_sem).start()

    def levels_here(n):
        lev_copy(n, core_peer, core_peer, csend_sem, crecv_sem).wait_recv()
        lev_copy(n, far, core_peer, fsend_sem, frecv_sem).wait_recv()

    lane48 = iota((48, LANES), 1)

    def sixteen_bands(c):
        band_messages(0, 15 if c == 0 else 16, c).wait_recv()
        rows = dot(expand[...], band_recv[16 * c : 16 * c + 16].reshape(512, LANES)).astype(BF16)
        for k in range(3):
            at = k * KROWS
            x0, x1, x2 = rows[at : at + 48], rows[at + 48 : at + 96], rows[at + 96 : at + 144]
            gathered[lev, c, at : at + 48, :] = jnp.where(lane48 < 64, x0, roll(x1, 64))
            gathered[lev, c, at + 48 : at + 96, :] = jnp.where(lane48 < 64, roll(x0, 64), x1)
            gathered[lev, c, at + 96 : at + 144, :] = x2
            if c == 2:
                send_levels(2 + k)

    lax.fori_loop(0, 8, prepare, 0)
    vert_copy.wait()

    for h in range(2):
        row = iota((384, COLS), 0)
        col = iota((384, COLS), 1)
        block = third(row >> 4)
        inside = row - 48 * block
        tile, w = col >> 7, col & 127
        u = jnp.where(tile < 2, tile, w >> 6)
        fld = jnp.where(tile < 2, w >> 6, 2)
        lvl = ((((w >> 1) & 3) - 2 * h - u) & 3) * 2 + ((w >> 4) & 1)
        m_sel[h] = onehot(
            (block == u * 4 + (w & 1) * 2 + ((w >> 5) & 1)) & (inside == fld * 16 + lvl * 2 + ((w >> 3) & 1))
        )
        row = iota((128, LANES), 0)
        w = iota((128, LANES), 1)
        lvl = ((((w >> 1) & 3) - 2 * h - (w >> 6)) & 3) * 2 + ((w >> 4) & 1)
        same = ((row >> 4) == (w >> 6) * 4 + (w & 1) * 2 + ((w >> 5) & 1)) & ((row & 1) == ((w >> 3) & 1))
        pair = ((row >> 1) & 7) * 8 + lvl
        weight = jnp.zeros((128, LANES), F32)
        for a in range(8):
            for c in range(a, 8):
                weight = jnp.where(pair == a * 8 + c, vert_ref[a : a + 1, c : c + 1], weight)
        weight = jnp.where(same, weight, 0.0)
        m_geo_hi[h] = weight.astype(BF16)
        m_geo_lo[h] = (weight - weight.astype(BF16).astype(F32)).astype(BF16)
    mine = band * SLOTS + iota((SLOTS, LANES), 0)
    owned = jnp.zeros((SLOTS, LANES), F32)
    for n in range(9):
        here = iota((SLOTS, LANES), 1) + LANES * n == mine
        owned = owned + jnp.where(here, waves_ref[n : n + 1, :].astype(F32), 0.0)
    owned = jnp.sum(owned, axis=1, keepdims=True)
    wave_col[...] = jnp.broadcast_to(owned, (SLOTS, LANES)).astype(jnp.int32)

    sixteen_bands(0)
    send_levels(0)
    lax.fori_loop(8, 16, prepare, 0)
    sixteen_bands(1)
    send_levels(1)
    forward(0)
    lax.fori_loop(16, 24, prepare, 0)
    sixteen_bands(2)
    forward(1)
    for n in range(2):
        levels_here(n)

    lane_j = iota((JPAD, LANES), 1)

    def grp_copy(k, d):
        to = (grp + d) % 4
        return pltpu.make_async_remote_copy(
            src_ref=grp_send.at[k, to], dst_ref=grp_recv.at[k, grp], send_sem=gsend_sem.at[k, d - 1],
            recv_sem=grecv_sem.at[k, d - 1], device_id={"grp": to}, device_id_type=MESH,
        )

    def finish(k):
        total = grp_send[k, grp].astype(F32)
        for d in range(1, 4):
            grp_copy(k, d).wait_recv()
            total = total + grp_recv[k, (grp + 4 - d) % 4].astype(F32)
        halves = 36 * (4 * lev + grp) + iota((64, JPAD), 1)
        for h in range(2):
            part = total[JPAD * h : JPAD * h + JPAD]
            hi = part.astype(BF16)
            lo = (part[:, 256:] - hi[:, 256:].astype(F32)).astype(BF16)
            plain = dot_nt(m_sel[h], hi)
            geo = dot_nt(m_geo_hi[h], hi[:, 256:]) + (
                dot_nt(m_geo_hi[h], lo) + dot_nt(m_geo_lo[h], hi[:, 256:])
            )
            for n in range(8):
                s, p = 8 * k + 4 * h + n // 2, n % 2
                values = jnp.concatenate([plain[48 * n : 48 * n + 48], geo[16 * n : 16 * n + 16]], axis=0)
                valid = wave_col[s : s + 1, :JPAD] + 2 * halves + p <= M - 1
                out_ref[s, p] = jnp.where(valid, values, 0.0).astype(BF16)[:, :36]

    group = (lane >> 1) & 3
    forward(2)
    for k in range(3):
        levels_here(2 + k)

        def blocks(rb, carry):
            c, o = rb // 3, rb % 3
            first = pl.multiple_of(16 * rb, 16)
            second = pl.multiple_of(KROWS + 16 * rb, 16)
            per_kind = []
            for f in range(3):
                at = pl.multiple_of(k * KROWS + 48 * f + 16 * o, 16)
                per_kind.append([gathered[n, c, pl.ds(at, 16), :] for n in range(4)])
            for n in range(4):
                picked = []
                for tiles in per_kind:
                    x = tiles[(3 - n) % 4]
                    for a in range(3):
                        x = jnp.where(group == a, tiles[(a - n) % 4], x)
                    picked.append(x)
                stat[n, pl.ds(first, 16), :LANES] = picked[0]
                stat[n, pl.ds(second, 16), :LANES] = picked[1]
                turned = roll(picked[2], 64)
                stat[n, pl.ds(first, 16), LANES:] = turned if n % 2 else picked[2]
                stat[n, pl.ds(second, 16), LANES:] = picked[2] if n % 2 else turned
            return carry

        lax.fori_loop(0, 9, blocks, 0)
        if k < 2:
            forward(3 + k)

        for n in range(8):
            prod[n] = dot(leg[8 * k + n], stat[n // 2])
        even = (lane_j & 1) == 0
        north = (lane_j & 32) == 0
        for g in range(4):
            halves = []
            for h in range(2):
                cols = []
                for n in (2 * h, 2 * h + 1):
                    for tile in range(2):
                        lanes = slice(LANES * tile, LANES * tile + LANES)
                        p0, p1 = slice(80 * g, 80 * g + 40), slice(80 * g + 40, 80 * g + 80)
                        cols.append(
                            jnp.where(
                                north,
                                jnp.where(even, prod[2 * n, p0, lanes], prod[2 * n + 1, p0, lanes]),
                                jnp.where(even, prod[2 * n, p1, lanes], prod[2 * n + 1, p1, lanes]),
                            )
                        )
                halves.append(jnp.concatenate([cols[0], cols[2], jnp.where(lane_j < 64, cols[1], cols[3])], axis=1))
            grp_send[k, g] = jnp.concatenate(halves, axis=0).astype(BF16)
        for d in (2, 1, 3):
            grp_copy(k, d).start()
        if k:
            finish(k - 1)
    finish(2)

    band_messages(0, BANDS - 1, 0).wait_send()
    for n in range(5):
        lev_copy(n, lev, y_peer, ysend_sem, yrecv_sem).wait_send()
        lev_copy(n, lev, core_peer, csend_sem, crecv_sem).wait_send()
        lev_copy(n, y_peer, core_peer, fsend_sem, frecv_sem).wait_send()
    for k in range(3):
        for d in range(1, 4):
            grp_copy(k, d).wait_send()


def body(fourier, legendre, lat_points, wave_slots, vertical):
    moved = jnp.transpose(fourier[:, :, :, :, 0], (0, 1, 2, 4, 3, 5)).reshape(72, 2, M)
    waves = wave_slots.reshape(9, LANES)
    hbm = pl.BlockSpec(memory_space=pltpu.HBM)
    vmem = pl.BlockSpec(memory_space=pltpu.VMEM)
    dma = pltpu.SemaphoreType.DMA
    out = pl.pallas_call(
        kernel,
        out_shape=pltpu.VMEM((SLOTS, 2, 64, 36), BF16),
        in_specs=[hbm] * 5,
        out_specs=vmem,
        scratch_shapes=[
            pltpu.VMEM((72, 2, M), BF16),
            pltpu.VMEM((1, 6), jnp.int32),
            pltpu.VMEM((9, LANES), jnp.int32),
            pltpu.VMEM((8, 8), F32),
            pltpu.VMEM((256, M), BF16),
            pltpu.VMEM((SLOTS, 2, KROWS, 288), BF16),
            pltpu.VMEM((SLOTS, 320, 288), BF16),
            pltpu.VMEM((288, 288), BF16),
            pltpu.VMEM((432, 512), BF16),
            pltpu.VMEM((BANDS, PACK, LANES), BF16),
            pltpu.VMEM((BANDS, PACK, LANES), BF16),
            pltpu.VMEM((4, 3, 432, LANES), BF16),
            pltpu.VMEM((4, 288, 256), BF16),
            pltpu.VMEM((8, 320, 256), F32),
            pltpu.VMEM((3, 4, 80, COLS), BF16),
            pltpu.VMEM((3, 4, 80, COLS), BF16),
            pltpu.VMEM((2, 384, COLS), BF16),
            pltpu.VMEM((2, 128, LANES), BF16),
            pltpu.VMEM((2, 128, LANES), BF16),
            pltpu.VMEM((296, 288), F32),
            pltpu.VMEM((SLOTS, LANES), jnp.int32),
            dma((4,)), dma, dma, dma((3,)),
            dma((5,)), dma((5,)), dma((5,)), dma((5,)), dma((5,)), dma((5,)),
            dma((3, 3)), dma((3, 3)),
        ],
        compiler_params=pltpu.CompilerParams(
            collective_id=0, has_side_effects=True, vmem_limit_bytes=62000000
        ),
        cost_estimate=pl.CostEstimate(flops=10**9, bytes_accessed=10**7, transcendentals=0),
    )(moved, lat_points, waves, vertical, legendre.reshape(SLOTS, 2, KROWS, 288))
    return out.reshape(SLOTS, 2, 4, 8, 2, 36)


def solution(mesh):
    placed = (
        P(None, "lev", None, None, "grp", "band", None),
        P("band", None, "lev", "grp", None),
        P("grp", "band"),
        P(),
        P(),
    )
    return jax.shard_map(
        body,
        mesh=mesh,
        in_specs=placed,
        out_specs=P("band", None, None, None, None, ("lev", "grp")),
        check_vma=False,
    )
```
